32 devices in a mesh: rep: 16 (over z, x, core), shard: 2 (over y).
Axes of the slice: x: 2, y: 2, z: 4, core: 2. Of those that a mesh axis runs over, the one named last changes fastest.
Arguments:
- tokens: bfloat16 [32768, 768], P(('rep', 'shard')), may hold values from -6 to 6
- cotangent: bfloat16 [32768, 768], P(('rep', 'shard')), may hold values from -6 to 6
- lengths: int32 [32], P(('rep', 'shard')), may hold values from 128 to 1024, as said below
- w_qkv: bfloat16 [768, 2304], P('shard'), may hold values from -0.21875 to 0.21875
- w_out: bfloat16 [768, 768], P('shard'), may hold values from -3.5 to 3.5
- w_up: bfloat16 [768, 3072], P('shard'), may hold values from -0.21875 to 0.21875
- w_down: bfloat16 [3072, 768], P('shard'), may hold values from -0.109375 to 0.109375
- norm_gains: bfloat16 [2, 768], P(None, 'shard'), may hold values from 0.5 to 1.5
- biases: bfloat16 [6, 768], P(None, 'shard'), may hold values from -3 to 3
- up_bias: bfloat16 [3072], P('shard'), may hold values from -3 to 3
Outputs:
- encoded: bfloat16 [32768, 768], P(('rep', 'shard'))
- grad_tokens: bfloat16 [32768, 768], P(('rep', 'shard'))
- grad_qkv: float32 [768, 2304], P('shard')
- grad_out: float32 [768, 768], P('shard')
- grad_up: float32 [768, 3072], P('shard')
- grad_down: float32 [3072, 768], P('shard')
- grad_gains: float32 [2, 768], P(None, 'shard')
- grad_biases: float32 [6, 768], P(None, 'shard')
- grad_up_bias: float32 [3072], P('shard')
The draws below stay inside these ranges and needn't reach their ends.
Inputs may be any that keep to these rules, and one draw needn't show every extreme that they name: Each sequence has lengths live tokens at the start of its 1024 slots; some sequence has exactly 1024.
All inputs are finite; a program needn't handle non-finite values.
Results may differ from the reference program's by a relative error of at most 0.02.
Values may be sent and summed in bfloat16 or wider, within the bound.
A program may use at most 192 MiB of HBM per device.

```python
import jax
import jax.numpy as jnp
from jax import lax

D = 768
HEADS = 12
HEAD_DIM = 64
FF = 3072
SEQ = 1024
LEN_MIN = 128
SLOTS = 1
SEQS = 32
TOKENS = 32768
N_REP = 16
N_SHARD = 2


def draw_lengths(key, part):
    first_key, second_key = jax.random.split(jax.random.fold_in(key, 11))
    drawn = jax.random.randint(first_key, (SEQS,), LEN_MIN, SEQ + 1)
    chosen = jax.random.randint(second_key, (), 0, SEQS)
    return jnp.where(jnp.arange(SEQS) == chosen, SEQ, drawn).astype(jnp.int32)


def levels(key, extent, shards, smallest, top_value):
    gain, own = 1.0, jax.random.fold_in(key, 6)
    for position, shards_of in shards:
        heights = jnp.exp(jax.random.uniform(jax.random.fold_in(own, position), (shards_of,), jnp.float32, smallest / len(shards), top_value / len(shards)))
        gain = gain * jnp.repeat(heights, extent[position] // shards_of).reshape([-1 if axis == position else 1 for axis in range(len(extent))])
    return gain


def gaussian(key, shape, spread, most, shards=(), kind=jnp.bfloat16):
    array = jax.random.normal(key, shape, jnp.float32) * spread
    if len(shards) > 0:
        array = levels(key, shape, shards, -0.22, 0.18) * array
    return jnp.clip(array, min=-most, max=most).astype(kind)


def setup_inputs(seed: int = 0) -> dict:
    key_list = jax.random.split(jax.random.key(seed), 11)
    tokens = gaussian(key_list[0], (TOKENS, D), 1.0, 6.0, ((0, 32),))
    cotangent = gaussian(key_list[1], (TOKENS, D), 1.0, 6.0, ((0, 32),))
    lengths = draw_lengths(jax.random.fold_in(key_list[10], 71), 0)
    w_qkv = gaussian(key_list[3], (D, 3 * D), D ** -0.5, 0.21875, ((0, 2),))
    w_out = gaussian(key_list[4], (D, D), (max(1, D // 256)) ** -0.5, 3.5, ((0, 2),))
    w_up = gaussian(key_list[5], (D, FF), D ** -0.5, 0.21875, ((0, 2),))
    w_down = gaussian(key_list[6], (FF, D), FF ** -0.5, 0.109375, ((0, 2),))
    norm_gains = jnp.clip(1.0 + 0.1 * jax.random.normal(key_list[7], (2, D), jnp.float32), 0.5, 1.5).astype(jnp.bfloat16)
    biases = gaussian(key_list[8], (6, D), 0.5, 3.0, ((1, 2),))
    up_bias = gaussian(key_list[9], (FF,), 0.5, 3.0, ((0, 2),))
    return dict(tokens=tokens, cotangent=cotangent, lengths=lengths, w_qkv=w_qkv, w_out=w_out, w_up=w_up, w_down=w_down, norm_gains=norm_gains, biases=biases, up_bias=up_bias)


@jax.custom_vjp
def low(v):
    return lax.optimization_barrier(v.astype(jnp.bfloat16)).astype(jnp.float32)

@jax.custom_vjp
def low_back(v):
    return v

def low_keep(v):
    return (low(v), None)

def low_pass(kept, grad):
    return (grad,)

def back_keep(v):
    return (v, None)

def back_low(kept, grad):
    return (low(grad),)
low.defvjp(low_keep, low_pass)
low_back.defvjp(back_keep, back_low)

def matmul_high(left, right):
    return jnp.dot(left, right, precision=lax.Precision.HIGHEST, preferred_element_type=jnp.float32)

def layer_norm(resid, gain_row, shift_row):
    center = resid - lax.optimization_barrier(jnp.mean(resid, -1, keepdims=True))
    variance = lax.optimization_barrier(jnp.mean(center * center, -1, keepdims=True))
    return center * lax.rsqrt(variance + 1e-12) * gain_row + shift_row

def encoder_layer(inputs_x, seq_lengths, w_qkv, w_out, w_up, w_down, norm_gains, biases, up_bias):
    seq_count = inputs_x.shape[0]
    flat_rows = inputs_x.reshape(seq_count * SEQ, D)
    qkv_bias = jnp.concatenate([biases[0], jnp.zeros_like(biases[0]), biases[1]])
    qkv_proj = low(low_back(matmul_high(flat_rows, w_qkv) + qkv_bias))
    queries = qkv_proj[:, :D].reshape(seq_count, SEQ, HEADS, HEAD_DIM)
    keys_all = qkv_proj[:, D:2 * D].reshape(seq_count, SEQ, HEADS, HEAD_DIM)
    values_all = qkv_proj[:, 2 * D:].reshape(seq_count, SEQ, HEADS, HEAD_DIM)
    scores = jnp.einsum('sqhd,skhd->shqk', queries, keys_all, precision=lax.Precision.HIGHEST) * HEAD_DIM ** (-0.5)
    scores = low_back(scores)
    positions = jnp.arange(SEQ).astype(jnp.int32)
    key_live = (positions[None, :] < seq_lengths.astype(jnp.int32)[:, None])[:, None, None, :]
    scores = jnp.where(key_live, scores, -1000000000.0)
    attn_probs = low(jax.nn.softmax(scores, axis=-1))
    attended = jnp.einsum('shqk,skhd->sqhd', attn_probs, values_all, precision=lax.Precision.HIGHEST)
    attended = low(low_back(attended.reshape(seq_count * SEQ, D)))
    branch = low_back(matmul_high(attended, w_out) + biases[2])
    normed_first = layer_norm(flat_rows + branch, norm_gains[0], biases[4])
    hidden_pre = low_back(matmul_high(low(normed_first), w_up) + up_bias)
    activated = low(jax.nn.gelu(hidden_pre, approximate=False))
    mlp_out = low_back(matmul_high(activated, w_down) + biases[3])
    result = layer_norm(normed_first + mlp_out, norm_gains[1], biases[5])
    return result.reshape(seq_count, SEQ, D)

def reference(tokens, cotangent, lengths, w_qkv, w_out, w_up, w_down, norm_gains, biases, up_bias):
    groups = N_REP * N_SHARD
    inputs_all = tokens.astype(jnp.float32).reshape(groups, SLOTS, SEQ, D)
    cot_all = cotangent.astype(jnp.float32).reshape(groups, SLOTS, SEQ, D)
    length_all = lengths.reshape(groups, SLOTS)
    params_all = tuple((param.astype(jnp.float32) for param in (w_qkv, w_out, w_up, w_down, norm_gains, biases, up_bias)))
    checkpointed = jax.checkpoint(encoder_layer)

    def scan_step(carried, group_item):
        inputs_x, seq_lengths, cot_group = group_item

        def forward_fn(inputs_in, *param_list):
            return checkpointed(inputs_in, seq_lengths, *param_list)
        outputs, backward_fn = jax.vjp(forward_fn, inputs_x, *params_all)
        grads_all = backward_fn(cot_group)
        carried = tuple((total + extra for total, extra in zip(carried, grads_all[1:])))
        return (carried, (outputs.astype(jnp.bfloat16), grads_all[0].astype(jnp.bfloat16)))
    initial = tuple((jnp.zeros_like(param) for param in params_all))
    summed, (encoded, grad_tokens) = lax.scan(scan_step, initial, (inputs_all, length_all, cot_all))
    return (encoded.reshape(TOKENS, D), grad_tokens.reshape(TOKENS, D), summed[0], summed[1], summed[2], summed[3], summed[4], summed[5], summed[6])
```

```python
import functools

import jax
import jax.numpy as jnp
from jax import lax
from jax.experimental import pallas as pl
from jax.experimental.pallas import tpu as pltpu
from jax.sharding import PartitionSpec as P

HEADS = 12
HEAD_DIM = 64
PAIR = 2 * HEAD_DIM

epsilon = 1e-12
masked_score = -1000000000.0
F32 = jnp.float32
BF16 = jnp.bfloat16


def dot_last(left, right):
    return lax.dot_general(left, right, (((1,), (1,)), ((), ())), preferred_element_type=F32)


def dot_plain(left, right):
    return lax.dot_general(left, right, (((1,), (0,)), ((), ())), preferred_element_type=F32)


def masked_keys(keys, length, head):
    lane = lax.broadcasted_iota(jnp.int32, keys.shape, 1)
    row = lax.broadcasted_iota(jnp.int32, keys.shape, 0)
    extra = jnp.where(row < length, 0.0, masked_score)
    return jnp.where(lane == (1 - head) * HEAD_DIM, extra, keys.astype(F32)).astype(BF16)


def head_lanes(block, head):
    lane = lax.broadcasted_iota(jnp.int32, block.shape, 1)
    inside = (lane >= head * HEAD_DIM) & (lane < (head + 1) * HEAD_DIM)
    return jnp.where(inside, block, 0.0)


def with_mask_lane(query, head):
    lane = lax.broadcasted_iota(jnp.int32, query.shape, 1)
    return jnp.where(lane == (1 - head) * HEAD_DIM, 1.0, query)


def forward_kernel(rows, length_ref, q_ref, k_ref, v_ref, out_ref, lse_ref, keys_aug, v_turned):
    seq = q_ref.shape[0]
    length = length_ref[pl.program_id(0)]
    for head in range(2):
        keys_aug[head] = masked_keys(k_ref[...], length, head)
    v_turned[...] = v_ref[...].T

    def block(index, _):
        span = pl.ds(pl.multiple_of(index * rows, rows), rows)
        scaled = q_ref[span, :].astype(F32) * HEAD_DIM ** (-0.5)
        parts = []
        for head in range(2):
            query = with_mask_lane(head_lanes(scaled, head), head).astype(BF16)
            scores = dot_last(keys_aug[head], query)
            top = jnp.max(scores, 0, keepdims=True)
            exponent = jnp.exp(scores - top)
            total = jnp.sum(exponent, 0, keepdims=True)
            mixed = dot_plain(
                v_turned[head * HEAD_DIM : (head + 1) * HEAD_DIM, :], exponent.astype(BF16)
            )
            parts.append(mixed / total)
            lse_ref[0, 0, pl.ds(head, 1), span] = top + jnp.log(total)
        out_ref[span, :] = jnp.concatenate(parts, 0).T.astype(BF16)
        return 0

    lax.fori_loop(0, seq // rows, block, 0)


def backward_kernel(
    rows,
    length_ref,
    q_ref,
    k_ref,
    v_ref,
    o_ref,
    do_ref,
    lse_ref,
    dq_ref,
    dk_ref,
    dv_ref,
    keys_aug,
    k_turned,
    dk_sum,
    dv_sum,
):
    seq = q_ref.shape[0]
    length = length_ref[pl.program_id(0)]
    for head in range(2):
        keys_aug[head] = masked_keys(k_ref[...], length, head)
    k_turned[...] = k_ref[...].T
    dk_sum[...] = jnp.zeros_like(dk_sum)
    dv_sum[...] = jnp.zeros_like(dv_sum)

    def block(index, _):
        span = pl.ds(pl.multiple_of(index * rows, rows), rows)
        scaled = q_ref[span, :].astype(F32) * HEAD_DIM ** (-0.5)
        grad = do_ref[span, :].astype(F32)
        product = (grad * o_ref[span, :].astype(F32)).T
        parts = []
        for head in range(2):
            lo, hi = head * HEAD_DIM, (head + 1) * HEAD_DIM
            alone = head_lanes(scaled, head)
            query = with_mask_lane(alone, head).astype(BF16)
            grad_low = head_lanes(grad, head).astype(BF16)
            inner = jnp.sum(product[lo:hi], 0, keepdims=True)
            lse = lse_ref[0, 0, pl.ds(head, 1), span]
            probs = jnp.exp(dot_last(keys_aug[head], query) - lse)
            dv_sum[...] += dot_plain(probs.astype(BF16), grad_low)
            grad_probs = dot_last(v_ref[...], grad_low)
            grad_scores = (probs * (grad_probs - inner)).astype(BF16)
            dk_sum[...] += dot_plain(grad_scores, alone.astype(BF16))
            parts.append(dot_plain(k_turned[lo:hi, :], grad_scores))
        dq_ref[span, :] = (jnp.concatenate(parts, 0).T * HEAD_DIM ** (-0.5)).astype(BF16)
        return 0

    lax.fori_loop(0, seq // rows, block, 0)
    dk_ref[...] = dk_sum[...].astype(BF16)
    dv_ref[...] = dv_sum[...].astype(BF16)


def column_spec(seq, offset):
    return pl.BlockSpec((seq, PAIR), lambda slot, pair: (slot, offset + pair))


def attention_forward(qkv_low, lengths, seq):
    tokens = qkv_low.shape[0]
    slots, pairs = tokens // seq, HEADS // 2
    return pl.pallas_call(
        functools.partial(forward_kernel, min(256, seq)),
        grid=(slots, pairs),
        in_specs=[
            pl.BlockSpec(memory_space=pltpu.SMEM),
            column_spec(seq, 0),
            column_spec(seq, pairs),
            column_spec(seq, 2 * pairs),
        ],
        out_specs=[
            column_spec(seq, 0),
            pl.BlockSpec((1, 1, 2, seq), lambda slot, pair: (slot, pair, 0, 0)),
        ],
        out_shape=[
            jax.ShapeDtypeStruct((tokens, HEADS * HEAD_DIM), BF16),
            jax.ShapeDtypeStruct((slots, pairs, 2, seq), F32),
        ],
        scratch_shapes=[pltpu.VMEM((2, seq, PAIR), BF16), pltpu.VMEM((PAIR, seq), BF16)],
        compiler_params=pltpu.CompilerParams(vmem_limit_bytes=48 * 2**20),
        cost_estimate=pl.CostEstimate(
            flops=16 * tokens * seq * HEADS * HEAD_DIM,
            bytes_accessed=8 * tokens * HEADS * HEAD_DIM,
            transcendentals=tokens * seq * HEADS,
        ),
        name="attention_forward",
    )(lengths, qkv_low, qkv_low, qkv_low)


def attention_backward(qkv_low, attended, d_attended, log_total, lengths, seq):
    tokens = qkv_low.shape[0]
    slots, pairs = tokens // seq, HEADS // 2
    grad_shape = jax.ShapeDtypeStruct((tokens, HEADS * HEAD_DIM), BF16)
    return pl.pallas_call(
        functools.partial(backward_kernel, min(256, seq)),
        grid=(slots, pairs),
        in_specs=[
            pl.BlockSpec(memory_space=pltpu.SMEM),
            column_spec(seq, 0),
            column_spec(seq, pairs),
            column_spec(seq, 2 * pairs),
            column_spec(seq, 0),
            column_spec(seq, 0),
            pl.BlockSpec((1, 1, 2, seq), lambda slot, pair: (slot, pair, 0, 0)),
        ],
        out_specs=[column_spec(seq, 0)] * 3,
        out_shape=[grad_shape] * 3,
        scratch_shapes=[
            pltpu.VMEM((2, seq, PAIR), BF16),
            pltpu.VMEM((PAIR, seq), BF16),
            pltpu.VMEM((seq, PAIR), F32),
            pltpu.VMEM((seq, PAIR), F32),
        ],
        compiler_params=pltpu.CompilerParams(vmem_limit_bytes=48 * 2**20),
        cost_estimate=pl.CostEstimate(
            flops=40 * tokens * seq * HEADS * HEAD_DIM,
            bytes_accessed=16 * tokens * HEADS * HEAD_DIM,
            transcendentals=tokens * seq * HEADS,
        ),
        name="attention_backward",
    )(lengths, qkv_low, qkv_low, qkv_low, attended, d_attended, log_total)


def swap(block, axis, count, bit):
    return lax.ppermute(block, axis, [(i, i ^ bit) for i in range(count)])


def bits_of(count):
    return [1 << i for i in range(count.bit_length() - 1)]


def join(mine, other, upper):
    return jnp.concatenate([jnp.where(upper, other, mine), jnp.where(upper, mine, other)], 0)


def after(value, earlier):
    return lax.optimization_barrier((value, earlier))[0]


def gather_shards(block, n_shard):
    me = lax.axis_index("shard")
    held = block[None]
    for bit in bits_of(n_shard):
        held = join(held, swap(held, "shard", n_shard, bit), (me & bit) != 0)
    return held


def gather_weight(piece, n_rep, n_shard, earlier):
    core = lax.axis_index("rep") & 1
    halves = piece.reshape(2, piece.shape[0] // 2, piece.shape[1])
    mine = lax.dynamic_index_in_dim(halves, core, 0, keepdims=False)
    if earlier is not None:
        mine = after(mine, earlier)
    held = gather_shards(mine, n_shard)
    other = swap(held, "rep", n_rep, 1)
    upper = core != 0
    whole = jnp.stack([jnp.where(upper, other, held), jnp.where(upper, held, other)], 1)
    return whole.reshape(n_shard * piece.shape[0], piece.shape[1]), held


def add_low(left, right):
    return (left.astype(F32) + right.astype(F32)).astype(BF16)


def halve(block, axis, count, bit, position):
    upper = (lax.axis_index(axis) & bit) != 0
    index = upper.astype(jnp.int32)
    keep = lax.dynamic_index_in_dim(block, index, position, keepdims=False)
    send = lax.dynamic_index_in_dim(block, 1 - index, position, keepdims=False)
    return add_low(keep, swap(send, axis, count, bit))


def reduce_gradient(grad, n_rep, n_shard):
    rows, cols = grad.shape
    rep = lax.axis_index("rep")
    part = rows // (2 * n_shard)
    held = halve(grad.reshape(n_shard, 2, part, cols), "rep", n_rep, 1, 1)
    for bit in reversed(bits_of(n_shard)):
        held = halve(
            held.reshape(2, held.shape[0] // 2, part, cols), "shard", n_shard, bit, 0
        )
    held = held[0]
    rest = bits_of(n_rep)[1:]
    for bit in rest:
        held = halve(held.reshape(2, held.shape[0] // 2, cols), "rep", n_rep, bit, 0)
    for bit in reversed(rest):
        held = join(held, swap(held, "rep", n_rep, bit), (rep & bit) != 0)
    return join(held, swap(held, "rep", n_rep, 1), (rep & 1) != 0).astype(F32)


def norm_forward(resid, gain_row, shift_row):
    center = resid - jnp.mean(resid, -1, keepdims=True)
    rstd_rows = lax.rsqrt(jnp.mean(center * center, -1, keepdims=True) + epsilon)
    normed = center * rstd_rows
    return (normed * gain_row + shift_row, normed, rstd_rows)


def norm_backward(grad_in, normed, rstd_rows, gain_row):
    scaled = grad_in * gain_row
    inner_term = (
        scaled
        - jnp.mean(scaled, -1, keepdims=True)
        - normed * jnp.mean(scaled * normed, -1, keepdims=True)
    )
    return (rstd_rows * inner_term, jnp.sum(grad_in * normed, 0), jnp.sum(grad_in, 0))


def gelu_pair(values):
    cdf = 0.5 + 0.5 * lax.erf(values * 0.7071067811865476)
    slope = cdf + values * (0.3989422804014327 * jnp.exp(-0.5 * values * values))
    return (values * cdf).astype(BF16), slope.astype(BF16)


def per_device(
    n_rep,
    n_shard,
    tokens,
    cotangent,
    lengths,
    w_qkv,
    w_out,
    w_up,
    w_down,
    norm_gains,
    biases,
    up_bias,
):
    width = tokens.shape[1]
    seq_len = tokens.shape[0] // lengths.shape[0]
    piece = width // n_shard
    gains, shifts = norm_gains.shape[0], biases.shape[0]
    small = jnp.concatenate([norm_gains.reshape(-1), biases.reshape(-1), up_bias])
    small_all = gather_shards(small[None], n_shard)[:, 0].astype(F32)
    cut = gains * piece
    end = cut + shifts * piece
    gain_f = jnp.swapaxes(small_all[:, :cut].reshape(n_shard, gains, piece), 0, 1)
    gain_f = gain_f.reshape(gains, width)
    bias_f = jnp.swapaxes(small_all[:, cut:end].reshape(n_shard, shifts, piece), 0, 1)
    bias_f = bias_f.reshape(shifts, width)
    upb_f = small_all[:, end:].reshape(-1)

    whole_qkv, mark = gather_weight(w_qkv, n_rep, n_shard, small_all)
    whole_out, mark = gather_weight(w_out, n_rep, n_shard, mark)
    whole_up, mark = gather_weight(w_up, n_rep, n_shard, mark)
    whole_down, mark = gather_weight(w_down, n_rep, n_shard, mark)

    qkv_bias = jnp.concatenate([bias_f[0], jnp.zeros_like(bias_f[0]), bias_f[1]])
    qkv_low = (jnp.dot(tokens, whole_qkv, preferred_element_type=F32) + qkv_bias).astype(BF16)
    attended_low, log_total = attention_forward(qkv_low, lengths, seq_len)
    branch = jnp.dot(attended_low, whole_out, preferred_element_type=F32) + bias_f[2]
    normed_first, unit_first, rstd_first = norm_forward(
        tokens.astype(F32) + branch, gain_f[0], bias_f[4]
    )
    normed_low = normed_first.astype(BF16)
    hidden_pre = jnp.dot(normed_low, whole_up, preferred_element_type=F32) + upb_f
    act_low, slope_low = gelu_pair(hidden_pre)
    mlp_out = jnp.dot(act_low, whole_down, preferred_element_type=F32) + bias_f[3]
    result, unit_second, rstd_second = norm_forward(normed_first + mlp_out, gain_f[1], bias_f[5])
    encoded = result.astype(BF16)

    d_second, d_gain_two, d_shift_two = norm_backward(
        cotangent.astype(F32), unit_second, rstd_second, gain_f[1]
    )
    d_mlp = d_second.astype(BF16)
    d_bias_down = jnp.sum(d_mlp.astype(F32), 0)
    grad_down = jnp.einsum("tf,td->fd", act_low, d_mlp, preferred_element_type=F32).astype(BF16)
    d_mlp = after(d_mlp, grad_down)
    d_act = jnp.einsum("td,fd->tf", d_mlp, whole_down, preferred_element_type=F32)
    d_pre = (d_act * slope_low.astype(F32)).astype(BF16)
    grad_up_bias = jnp.sum(d_pre.astype(F32), 0)
    grad_up = jnp.einsum("td,tf->df", normed_low, d_pre, preferred_element_type=F32).astype(BF16)
    d_pre = after(d_pre, grad_up)
    d_normed = d_second + jnp.einsum("tf,df->td", d_pre, whole_up, preferred_element_type=F32)
    d_first, d_gain_one, d_shift_one = norm_backward(d_normed, unit_first, rstd_first, gain_f[0])
    d_branch = d_first.astype(BF16)
    d_bias_out = jnp.sum(d_branch.astype(F32), 0)
    grad_out = jnp.einsum("ta,td->ad", attended_low, d_branch, preferred_element_type=F32)
    grad_out = grad_out.astype(BF16)
    d_branch = after(d_branch, grad_out)
    d_attended = jnp.einsum("td,ad->ta", d_branch, whole_out, preferred_element_type=F32)
    d_query, d_keys, d_values = attention_backward(
        qkv_low, attended_low, d_attended.astype(BF16), log_total, lengths, seq_len
    )
    d_qkv = jnp.concatenate([d_query, d_keys, d_values], axis=1)
    grad_qkv = jnp.einsum("td,te->de", tokens, d_qkv, preferred_element_type=F32).astype(BF16)
    d_qkv = after(d_qkv, grad_qkv)
    d_qkv_sums = jnp.sum(d_qkv.astype(F32), 0)
    grad_tokens = (
        d_first + jnp.einsum("te,de->td", d_qkv, whole_qkv, preferred_element_type=F32)
    ).astype(BF16)

    sum_down = reduce_gradient(grad_down, n_rep, n_shard)
    sum_up = reduce_gradient(grad_up, n_rep, n_shard)
    sum_out = reduce_gradient(grad_out, n_rep, n_shard)
    sum_qkv = reduce_gradient(grad_qkv, n_rep, n_shard)

    rows = [
        d_gain_one,
        d_gain_two,
        d_qkv_sums[:width],
        d_qkv_sums[2 * width :],
        d_bias_out,
        d_bias_down,
        d_shift_one,
        d_shift_two,
    ]
    small_sum = lax.psum(jnp.concatenate(rows + [grad_up_bias]), ("rep", "shard"))
    me = lax.axis_index("shard")
    table = small_sum[: len(rows) * width].reshape(len(rows), width)
    table = lax.dynamic_slice_in_dim(table, me * piece, piece, 1)
    up_piece = lax.dynamic_slice_in_dim(
        small_sum[len(rows) * width :], me * up_bias.shape[0], up_bias.shape[0], 0
    )
    return (
        encoded,
        grad_tokens,
        sum_qkv,
        sum_out,
        sum_up,
        sum_down,
        table[:gains],
        table[gains:],
        up_piece,
    )


def solution(mesh):
    both = P(("rep", "shard"), None)
    rows = P("shard", None)
    columns = P(None, "shard")
    in_specs = (both, both, P(("rep", "shard")), rows, rows, rows, rows, columns, columns, P("shard"))
    out_specs = (both, both, rows, rows, rows, rows, columns, columns, P("shard"))
    return jax.shard_map(
        functools.partial(per_device, mesh.shape["rep"], mesh.shape["shard"]),
        mesh=mesh,
        in_specs=in_specs,
        out_specs=out_specs,
        check_vma=False,
    )
```
